32 devices in a mesh: grp: 2 (over x), tmpl: 16 (over z, y, core).
Axes of the slice: x: 2, y: 2, z: 4, core: 2. Of those that a mesh axis runs over, the one named last changes fastest.
Arguments:
- strain: float32 [16, 512, 1024], P('grp', None, 'tmpl'), parts along dimension 0, may hold values from -6 to 6
- analysis: float32 [1024, 1024], P('grp', 'tmpl'), parts along dimension 0, may hold values from -6 to 6
- bank: bfloat16 [2, 16, 512, 512], P(None, None, 'tmpl'), may hold values from -6 to 6
- cutoff: int32 [16], replicated, may hold values from 65536 to 262144
- order: int32 [16], replicated, may hold values from 0 to 15, each once
Outputs:
- snr: bfloat16 [32, 512, 1024], P(('grp', 'tmpl')), parts along dimension 0
The draws below stay inside these ranges and needn't reach their ends.
There are 2 independent parts, one for each index of `grp`. The reference program is written for one: setup_inputs(seed, part) draws one part's arguments, and reference() takes and returns one part's arrays. A program takes and returns all parts, laid end to end along the dimension named above; an argument that names none is the same for every part. Nothing has to cross between parts.
Inputs may be any that keep to these rules, and one draw needn't show every extreme that they name: `order`: a permutation of the bank's templates.
All inputs are finite; a program needn't handle non-finite values.
Results may differ from the reference program's by a relative error of at most 0.013.
Values may be sent and summed in bfloat16 or wider, within the bound.
A program may use at most 64 MiB of HBM per device.

```python
import math
import jax
import jax.numpy as jnp
from jax import lax

N1 = 512
N2 = 1024
SEGS = 8
SAMPLES = 524288
TEMPLATES = 16


def plant(result, own_key, least, top_value):
    spot = [jax.random.randint(jax.random.fold_in(own_key, axis), (), 0, length) for axis, length in enumerate(result.shape)]
    longest = result.shape.index(max(result.shape))
    next_to = spot[:longest] + [(spot[longest] + 1) % result.shape[longest]] + spot[longest + 1:]
    return result.at[tuple(spot)].set(least).at[tuple(next_to)].set(top_value)


def steps_of(key, dims, cuts, least, high):
    level, own = 1.0, jax.random.fold_in(key, 6)
    for axis_at, blocks in cuts:
        steps = jnp.exp(jax.random.uniform(jax.random.fold_in(own, axis_at), (blocks,), jnp.float32, least / len(cuts), high / len(cuts)))
        level = level * jnp.repeat(steps, dims[axis_at] // blocks).reshape([-1 if axis == axis_at else 1 for axis in range(len(dims))])
    return level


def normal_values(stream_key, shape, scale, limit, shards=(), kind=jnp.bfloat16):
    loudness = steps_of(stream_key, shape, shards, -0.22, 0.18) if shards else 1.0
    drawn = jax.random.normal(stream_key, shape, jnp.float32) * scale * loudness
    return jnp.minimum(jnp.maximum(drawn, -limit), limit).astype(kind)


def setup_inputs(seed: int = 0, part: int = 0) -> dict:
    streams_of = jax.random.split(jax.random.key(seed), 6)
    part_splits = jax.random.split(jax.random.fold_in(streams_of[5], part), 6)
    return {
        "strain": normal_values(part_splits[0], (SEGS, N1, N2), 1.0, 6.0, ((2, 16),), jnp.float32),
        "analysis": normal_values(part_splits[1], (N1, N2), 1.0, 6.0, ((1, 16),), jnp.float32),
        "bank": normal_values(streams_of[2], (2, TEMPLATES, N1, N2 // 2), 1.0, 6.0, ((2, 16),)),
        "cutoff": plant(jax.random.randint(streams_of[3], (TEMPLATES,), SAMPLES // 8, SAMPLES // 2 + 1), jax.random.fold_in(streams_of[3], 1), SAMPLES // 8, (SAMPLES // 2 + 1) - 1).astype(jnp.int32),
        "order": jax.random.permutation(streams_of[4], TEMPLATES).astype(jnp.int32),
    }


def angles(left_idx, right_idx, period):
    product = left_idx[:, None] * right_idx[None, :] % period
    phase_angle = product.astype(jnp.float32) * (2.0 * math.pi / period)
    return (jnp.cos(phase_angle), jnp.sin(phase_angle))

def round_trip(values):
    narrow = lax.optimization_barrier(values.astype(jnp.bfloat16))
    return narrow.astype(jnp.float32)

def reference(strain, analysis, bank, cutoff, order):
    length = N1 * N2
    half_len = N2 // 2
    sample_idx = jnp.arange(length, dtype=jnp.int32)
    window = math.sqrt(8.0 / 3.0) * jnp.sin(sample_idx.astype(jnp.float32) * (math.pi / length)) ** 2
    series = jnp.concatenate([strain.reshape(SEGS, length) * window, analysis.reshape(1, length)], 0)
    spectra = jnp.fft.fft(series, axis=1).reshape(SEGS + 1, N2, N1)[:, :half_len, :].transpose(0, 2, 1)
    spec_real = jnp.real(spectra).astype(jnp.float32)
    spec_imag = jnp.imag(spectra).astype(jnp.float32)
    power_spec = jnp.maximum(lax.optimization_barrier(jnp.mean(spec_real[:SEGS] ** 2 + spec_imag[:SEGS] ** 2, axis=0)), 0.2 * length)
    white_real = round_trip(spec_real[SEGS] / power_spec)
    white_imag = round_trip(spec_imag[SEGS] / power_spec)
    freq_bin = jnp.arange(N1, dtype=jnp.int32)[:, None] + N1 * jnp.arange(half_len, dtype=jnp.int32)[None, :]
    chosen = jnp.take(bank, order, axis=1).transpose(1, 0, 2, 3)
    cuts = jnp.take(cutoff, order)
    cos_twist, sin_twist = angles(jnp.arange(N1, dtype=jnp.int32), jnp.arange(N2, dtype=jnp.int32), length)

    def one_template(item):
        pair, cut_bin = item
        tmpl_real = pair[0].astype(jnp.float32)
        tmpl_imag = pair[1].astype(jnp.float32)
        in_band = freq_bin < cut_bin
        norm_sq = jnp.sum(jnp.where(in_band, (tmpl_real ** 2 + tmpl_imag ** 2) / power_spec, 0.0))
        filt_real = round_trip(jnp.where(in_band, white_real * tmpl_real + white_imag * tmpl_imag, 0.0))
        filt_imag = round_trip(jnp.where(in_band, white_imag * tmpl_real - white_real * tmpl_imag, 0.0))
        padded = jnp.pad(filt_real + 1j * filt_imag, ((0, 0), (0, N2 - half_len)))
        spread = N2 * jnp.fft.ifft(padded, axis=1)
        spread_real = jnp.real(spread)
        spread_imag = jnp.imag(spread)
        lift_real = round_trip(spread_real * cos_twist - spread_imag * sin_twist)
        lift_imag = round_trip(spread_real * sin_twist + spread_imag * cos_twist)
        field = N1 * jnp.fft.ifft(lift_real + 1j * lift_imag, axis=0)
        return (jnp.abs(field) / jnp.sqrt(norm_sq)).astype(jnp.bfloat16)
    return lax.map(one_template, (chosen, cuts))
```

```python
import functools
import math

import jax
import jax.numpy as jnp
import numpy as np
from jax import lax
from jax.experimental import pallas as pl
from jax.experimental.pallas import tpu as pltpu
from jax.sharding import PartitionSpec as P


def angles(left_idx, right_idx, period):
    product = left_idx[:, None] * right_idx[None, :] % period
    phase_angle = product.astype(jnp.float32) * (2.0 * math.pi / period)
    return (jnp.cos(phase_angle), jnp.sin(phase_angle))


def filtered(white_pair, tmpl_pair, cut_bins, freq_bin):
    white_real = white_pair[0].astype(jnp.float32)
    white_imag = white_pair[1].astype(jnp.float32)
    tmpl_real = tmpl_pair[0].astype(jnp.float32)
    tmpl_imag = tmpl_pair[1].astype(jnp.float32)
    in_band = freq_bin[None] < cut_bins[:, None, None]
    filt_real = jnp.where(in_band, white_real * tmpl_real + white_imag * tmpl_imag, 0.0)
    filt_imag = jnp.where(in_band, white_imag * tmpl_real - white_real * tmpl_imag, 0.0)
    return jnp.concatenate([filt_real, filt_imag], -1).astype(jnp.bfloat16)


def inverse_rows(stacked, row_bins, second_len, length):
    half_len = second_len // 2
    cosine, sine = angles(
        jnp.arange(half_len, dtype=jnp.int32), jnp.arange(second_len, dtype=jnp.int32), second_len
    )
    dft_table = jnp.concatenate(
        [jnp.concatenate([cosine, sine], 1), jnp.concatenate([-sine, cosine], 1)], 0
    ).astype(jnp.bfloat16)
    spread = jnp.einsum("tkf,fg->tkg", stacked, dft_table, preferred_element_type=jnp.float32)
    spread_real = spread[..., :second_len]
    spread_imag = spread[..., second_len:]
    cos_twist, sin_twist = angles(row_bins, jnp.arange(second_len, dtype=jnp.int32), length)
    lift_real = spread_real * cos_twist - spread_imag * sin_twist
    lift_imag = spread_real * sin_twist + spread_imag * cos_twist
    return jnp.concatenate([lift_real, lift_imag], -1).astype(jnp.bfloat16)


def inverse_cols(lifted, first_len, second_len):
    row_idx = jnp.arange(first_len, dtype=jnp.int32)
    cosine, sine = angles(row_idx, row_idx, first_len)
    cosine = cosine.astype(jnp.bfloat16)
    sine = sine.astype(jnp.bfloat16)
    lift_real = lifted[..., :second_len]
    lift_imag = lifted[..., second_len:]
    field_real = jnp.einsum(
        "ak,tkb->tab", cosine, lift_real, preferred_element_type=jnp.float32
    ) - jnp.einsum("ak,tkb->tab", sine, lift_imag, preferred_element_type=jnp.float32)
    field_imag = jnp.einsum(
        "ak,tkb->tab", sine, lift_real, preferred_element_type=jnp.float32
    ) + jnp.einsum("ak,tkb->tab", cosine, lift_imag, preferred_element_type=jnp.float32)
    return (field_real, field_imag)


def local(strain, analysis, bank, cutoff, order):
    highest = lax.Precision.HIGHEST
    dev_count = lax.axis_size("tmpl")
    my_index = lax.axis_index("tmpl")
    seg_count = strain.shape[0]
    first_len = strain.shape[1]
    col_count = strain.shape[2]
    second_len = col_count * dev_count
    length = first_len * second_len
    half_len = second_len // 2
    row_count = first_len // dev_count
    row_idx = jnp.arange(first_len, dtype=jnp.int32)
    col_index = my_index * col_count + jnp.arange(col_count, dtype=jnp.int32)
    sample_idx = row_idx[:, None] * second_len + col_index[None, :]
    window = (
        math.sqrt(8.0 / 3.0) * jnp.sin(sample_idx.astype(jnp.float32) * (math.pi / length)) ** 2
    )
    series = jnp.concatenate([strain * window, analysis[None]], 0)
    cos_one, sin_one = angles(row_idx, row_idx, first_len)
    part_real = jnp.einsum("ka,sab->skb", cos_one, series, precision=highest)
    part_imag = -jnp.einsum("ka,sab->skb", sin_one, series, precision=highest)
    cos_twist, sin_twist = angles(row_idx, col_index, length)
    twist_real = part_real * cos_twist + part_imag * sin_twist
    twist_imag = part_imag * cos_twist - part_real * sin_twist
    moved = lax.all_to_all(
        jnp.stack([twist_real, twist_imag]).astype(jnp.bfloat16),
        "tmpl",
        split_axis=2,
        concat_axis=3,
        tiled=True,
    ).astype(jnp.float32)
    cos_two, sin_two = angles(
        jnp.arange(second_len, dtype=jnp.int32), jnp.arange(half_len, dtype=jnp.int32), second_len
    )
    spec_real = jnp.einsum("skb,bf->skf", moved[0], cos_two, precision=highest) + jnp.einsum(
        "skb,bf->skf", moved[1], sin_two, precision=highest
    )
    spec_imag = jnp.einsum("skb,bf->skf", moved[1], cos_two, precision=highest) - jnp.einsum(
        "skb,bf->skf", moved[0], sin_two, precision=highest
    )
    power_spec = jnp.maximum(
        jnp.mean(spec_real[:seg_count] ** 2 + spec_imag[:seg_count] ** 2, axis=0), 0.2 * length
    )
    whitened = jnp.stack(
        [spec_real[seg_count] / power_spec, spec_imag[seg_count] / power_spec]
    ).astype(jnp.bfloat16)
    own_rows = my_index * row_count + jnp.arange(row_count, dtype=jnp.int32)
    half_idx = jnp.arange(half_len, dtype=jnp.int32)
    freq_local = own_rows[:, None] + first_len * half_idx[None, :]
    pick = (order[:, None] == jnp.arange(order.shape[0], dtype=jnp.int32)[None, :]).astype(bank.dtype)
    chosen = jnp.einsum("jt,ctkf->cjkf", pick, bank)
    cuts = jnp.take(cutoff, order)
    bank_real = chosen[0].astype(jnp.float32)
    bank_imag = chosen[1].astype(jnp.float32)
    in_band = freq_local[None] < cuts[:, None, None]
    local_norm = jnp.sum(
        jnp.where(in_band, (bank_real**2 + bank_imag**2) / power_spec, 0.0), axis=(1, 2)
    )
    norm_sq = lax.psum(local_norm, "tmpl")
    per_device = cuts.shape[0] // dev_count
    own_norm = lax.dynamic_slice_in_dim(norm_sq, my_index * per_device, per_device)
    stacked = filtered(whitened, chosen, cuts, freq_local)
    lifted = lax.all_to_all(
        inverse_rows(stacked, own_rows, second_len, length),
        "tmpl",
        split_axis=0,
        concat_axis=1,
        tiled=True,
    )
    field_real, field_imag = inverse_cols(lifted, first_len, second_len)
    magnitude = jnp.sqrt(field_real**2 + field_imag**2)
    return (magnitude / jnp.sqrt(own_norm)[:, None, None]).astype(jnp.bfloat16)


def unit(left, right, period):
    phase = (left[:, None] * right[None, :] % period) * (2.0 * np.pi / period)
    return np.cos(phase), np.sin(phase)


def tables(devs, first, cols):
    second = cols * devs
    half = second // 2
    length = first * second
    rows = first // devs
    k1 = np.arange(first, dtype=np.int64)
    b = np.arange(second, dtype=np.int64)
    cos, sin = unit(k1, k1, first)
    fwd_one = np.stack([cos.reshape(devs, rows, first), sin.reshape(devs, rows, first)], 1)
    fwd_one = fwd_one.reshape(devs, 2 * rows, first)
    samples = k1[:, None] * second + b[None, :]
    window = np.sqrt(8.0 / 3.0) * np.sin(samples * (np.pi / length)) ** 2
    tcos, tsin = unit(k1, b, length)

    def paired(left, right):
        split = [part.reshape(first, devs, cols).transpose(1, 0, 2) for part in (left, right)]
        return np.concatenate(split, 2)

    window = paired(window, window)
    twist_cos = paired(tcos, tcos)
    twist_sin = paired(tsin, -tsin)
    low = np.arange(half, dtype=np.int64)
    blocks = []
    for bins in (low, second - 1 - low):
        cos, sin = unit(b, bins, second)
        real = np.concatenate([cos.reshape(devs, cols, half), sin.reshape(devs, cols, half)], 1)
        imag = np.concatenate([-sin.reshape(devs, cols, half), cos.reshape(devs, cols, half)], 1)
        blocks += [real.reshape(2 * second, half), imag.reshape(2 * second, half)]
    fwd_two = np.concatenate(blocks, 1)
    cos, sin = unit(low, b, second)
    inv_one = np.block([[cos, sin], [-sin, cos]])
    cos, sin = unit(k1, k1, first)
    inv_two = np.block([[cos, -sin], [sin, cos]])
    found = (fwd_one, window, twist_cos, twist_sin, fwd_two, inv_one, tcos, tsin, inv_two)
    return [part.astype(np.float32).astype(jnp.bfloat16) for part in found]


def kernel(
    devs, group,
    cutoff, order, strain_h, analysis_h, bank_h, one_h, window_h, tcos_h, tsin_h, two_h, inv_h, ucos_h, usin_h, last_h,
    out,
    strain, analysis, bank, one, window, tcos, tsin, two, inv, ucos, usin, last,
    series, send_a, recv_a, spec, mirror_out, mirror_in, edge_out, edge_in, send_q, recv_q, norm_out, norm_in, lifted,
    load_sem, a_send, a_recv, m_send, m_recv, q_send, q_recv, n_send, n_recv,
):
    f32, bf16 = jnp.float32, jnp.bfloat16
    me = lax.axis_index("tmpl")
    segs, first, cols = strain.shape
    pairs = segs // 2
    width = 2 * cols
    rows = first // devs
    second = cols * devs
    half = second // 2
    length = first * second
    packed = pairs * rows

    loads = []
    for at, (src, dst) in enumerate([
        (strain_h, strain), (analysis_h, analysis), (window_h.at[me], window), (one_h, one),
        (tcos_h.at[me], tcos), (tsin_h.at[me], tsin), (two_h, two), (bank_h, bank),
        (inv_h, inv), (ucos_h, ucos), (usin_h, usin), (last_h, last),
    ]):
        copy = pltpu.make_async_copy(src, dst, load_sem.at[at])
        copy.start()
        loads.append(copy)

    barrier = pltpu.get_barrier_semaphore()

    def greet(step, carry):
        pl.semaphore_signal(barrier, inc=1, device_id={"tmpl": lax.rem(me + step, devs)},
                            device_id_type=pl.DeviceIdType.MESH)
        return carry

    lax.fori_loop(1, devs, greet, 0)

    for copy in loads[:6]:
        copy.wait()
    for pair in range(pairs):
        both = jnp.concatenate([strain[2 * pair], strain[2 * pair + 1]], 1)
        series[:, pair * width:(pair + 1) * width] = (both * window[...].astype(f32)).astype(bf16)
    series[:, pairs * width:] = jnp.concatenate(
        [analysis[...], jnp.zeros((first, cols), f32)], 1).astype(bf16)
    lane = lax.broadcasted_iota(jnp.int32, (rows, width), 1)
    sign = jnp.where(lane < cols, -1.0, 1.0)

    pl.semaphore_wait(barrier, devs - 1)

    def a_copy(peer, source):
        return pltpu.make_async_remote_copy(
            src_ref=send_a.at[peer],
            dst_ref=recv_a.at[:, pl.ds(pl.multiple_of(source * width, width), width)],
            send_sem=a_send.at[peer], recv_sem=a_recv.at[source],
            device_id={"tmpl": peer}, device_id_type=pl.DeviceIdType.MESH)

    own_set = me // group
    sets = devs // group

    def spread(step, carry):
        chunk = lax.rem(own_set + 1 + step, sets)
        part = jnp.dot(one[pl.ds(chunk * group, group)].reshape(group * 2 * rows, first), series[...],
                       preferred_element_type=f32)
        for member in range(group):
            peer = chunk * group + member
            at = pl.ds(pl.multiple_of(peer * rows, rows), rows)
            cos, sin = tcos[at, :].astype(f32), tsin[at, :].astype(f32)
            base = member * 2 * rows
            for seg in range(pairs + 1):
                upper = part[base:base + rows, seg * width:(seg + 1) * width]
                lower = part[base + rows:base + 2 * rows, seg * width:(seg + 1) * width]
                field = upper + pltpu.roll(lower * sign, cols, 1)
                field = field * cos + pltpu.roll(field, cols, 1) * sin
                send_a[peer, seg * rows:(seg + 1) * rows, :] = field.astype(bf16)

            @pl.when(peer != me)
            def _():
                a_copy(peer, me).start()
        return carry

    lax.fori_loop(0, sets, spread, 0)
    recv_a[:, pl.ds(pl.multiple_of(me * width, width), width)] = send_a[me]
    loads[6].wait()

    def others(body):
        def step(at, carry):
            body(lax.rem(me + at, devs))
            return carry
        lax.fori_loop(1, devs, step, 0)

    others(lambda peer: a_copy(peer, peer).wait_recv())

    chunk_cols = min(half, 512)

    def columns(step, carry):
        at = pl.ds(pl.multiple_of(step * chunk_cols, chunk_cols), chunk_cols)
        spec[:, at] = jnp.dot(recv_a[...], two[:, at], preferred_element_type=f32)
        return carry

    lax.fori_loop(0, 2 * second // chunk_cols, columns, 0)

    def power(start):
        total = jnp.zeros((rows, half), f32)
        for pair in range(pairs):
            for part in (start, start + half):
                value = spec[pair * rows:(pair + 1) * rows, part:part + half]
                total = total + value * value
        return total

    far = power(second)
    near_row = lax.broadcasted_iota(jnp.int32, (rows, rows), 0)
    near_col = lax.broadcasted_iota(jnp.int32, (rows, rows), 1)
    flip = jnp.where(near_row + near_col == rows, 1.0, 0.0)
    mirror_out[...] = jnp.dot(flip, far, preferred_element_type=f32, precision=lax.Precision.HIGHEST)
    edge_out[...] = far[:8]
    partner = devs - 1 - me
    edge_partner = lax.rem(devs - me, devs)
    mirror_copy = pltpu.make_async_remote_copy(
        src_ref=mirror_out, dst_ref=mirror_in, send_sem=m_send.at[0], recv_sem=m_recv.at[0],
        device_id={"tmpl": partner}, device_id_type=pl.DeviceIdType.MESH)
    edge_copy = pltpu.make_async_remote_copy(
        src_ref=edge_out, dst_ref=edge_in, send_sem=m_send.at[1], recv_sem=m_recv.at[1],
        device_id={"tmpl": edge_partner}, device_id_type=pl.DeviceIdType.MESH)
    mirror_copy.start()

    @pl.when(edge_partner != me)
    def _():
        edge_copy.start()
    close = power(0)

    @pl.when(edge_partner == me)
    def _():
        edge_lane = lax.broadcasted_iota(jnp.int32, (8, half), 1)
        shifted = jnp.where(edge_lane == 0, close[:8], pltpu.roll(far[:8], 1, 1))
        edge_in[...] = jnp.where(me == 0, shifted, far[:8])

    @pl.when(edge_partner != me)
    def _():
        edge_copy.wait_recv()
    mirror_copy.wait_recv()
    row = lax.broadcasted_iota(jnp.int32, (rows, half), 0)
    opposite = jnp.where(row == 0, edge_in[0:1, :], mirror_in[...])
    inverse = 1.0 / jnp.maximum((close + opposite) * (0.5 / segs), 0.2 * length)
    white_real = (spec[packed:, :half] * inverse).astype(bf16).astype(f32)
    white_imag = (spec[packed:, half:second] * inverse).astype(bf16).astype(f32)
    freq = me * rows + row + first * lax.broadcasted_iota(jnp.int32, (rows, half), 1)
    loads[7].wait()

    def q_copy(peer, source):
        return pltpu.make_async_remote_copy(
            src_ref=send_q.at[peer],
            dst_ref=recv_q.at[pl.ds(pl.multiple_of(source * rows, rows), rows), :],
            send_sem=q_send.at[peer], recv_sem=q_recv.at[source],
            device_id={"tmpl": peer}, device_id_type=pl.DeviceIdType.MESH)

    def n_copy(peer, source):
        return pltpu.make_async_remote_copy(
            src_ref=norm_out.at[peer], dst_ref=norm_in.at[source],
            send_sem=n_send.at[peer], recv_sem=n_recv.at[source],
            device_id={"tmpl": peer}, device_id_type=pl.DeviceIdType.MESH)

    def filters(step, carry):
        peer = lax.rem(me + step, devs)
        which = order[peer]
        inside = freq < cutoff[which]
        real, imag = bank[0, which].astype(f32), bank[1, which].astype(f32)
        send_q[peer, :, :half] = jnp.where(inside, white_real * real + white_imag * imag, 0.0).astype(bf16)
        send_q[peer, :, half:] = jnp.where(inside, white_imag * real - white_real * imag, 0.0).astype(bf16)
        weight = jnp.where(inside, (real * real + imag * imag) * inverse, 0.0)
        total = sum(weight[at:at + 8] for at in range(0, rows, 8))
        norm_out[peer] = sum(total[:, at:at + 128] for at in range(0, half, 128))

        @pl.when(peer != me)
        def _():
            q_copy(peer, me).start()
            n_copy(peer, me).start()
        return carry

    lax.fori_loop(1, devs + 1, filters, 0)
    recv_q[pl.ds(pl.multiple_of(me * rows, rows), rows), :] = send_q[me]
    norm_in[me] = norm_out[me]
    for copy in loads[8:]:
        copy.wait()

    def rows_back(step, carry):
        chunk = lax.rem(own_set + step, sets)
        for member in range(group):
            peer = chunk * group + member

            @pl.when(peer != me)
            def _():
                q_copy(peer, peer).wait_recv()
        at = pl.ds(pl.multiple_of(chunk * group * rows, group * rows), group * rows)
        below = pl.ds(pl.multiple_of(first + chunk * group * rows, group * rows), group * rows)
        wide = jnp.dot(recv_q[at, :], inv[...], preferred_element_type=f32)
        real, imag = wide[:, :second], wide[:, second:]
        cos, sin = ucos[at, :].astype(f32), usin[at, :].astype(f32)
        lifted[at, :] = (real * cos - imag * sin).astype(bf16)
        lifted[below, :] = (real * sin + imag * cos).astype(bf16)
        return carry

    lax.fori_loop(0, sets, rows_back, 0)
    others(lambda peer: n_copy(peer, peer).wait_recv())
    norm = jnp.sum(jnp.sum(jnp.sum(norm_in[...], 0), 0, keepdims=True), 1, keepdims=True)
    gain = 1.0 / jnp.sqrt(norm)
    tail = 256

    def cols_back(step, carry):
        at = pl.ds(pl.multiple_of(step * tail, tail), tail)
        field = jnp.dot(last[...], lifted[:, at], preferred_element_type=f32)
        real, imag = field[:first], field[first:]
        out[0, :, at] = (jnp.sqrt(real * real + imag * imag) * gain).astype(bf16)
        return carry

    lax.fori_loop(0, second // tail, cols_back, 0)

    def drain(peer):
        a_copy(peer, me).wait_send()
        q_copy(peer, me).wait_send()
        n_copy(peer, me).wait_send()

    others(drain)
    mirror_copy.wait_send()

    @pl.when(edge_partner != me)
    def _():
        edge_copy.wait_send()


def fused(strain, analysis, bank, cutoff, order):
    devs = lax.axis_size("tmpl")
    segs, first, cols = strain.shape
    second = cols * devs
    half = second // 2
    rows = first // devs
    group = 4
    parts = segs // 2 + 1
    f32, bf16 = jnp.float32, jnp.bfloat16
    consts = [jnp.asarray(part) for part in tables(devs, first, cols)]
    smem = pl.BlockSpec(memory_space=pltpu.SMEM)
    held = [strain, analysis, bank] + consts
    shapes = [part.shape for part in held]
    for at in (4, 5, 6):
        shapes[at] = shapes[at][1:]
    vmem = pltpu.VMEM
    dma = pltpu.SemaphoreType.DMA
    return pl.pallas_call(
        functools.partial(kernel, devs, group),
        out_shape=jax.ShapeDtypeStruct((1, first, second), bf16),
        in_specs=[smem, smem] + [pl.BlockSpec(memory_space=pl.ANY)] * len(held),
        out_specs=pl.BlockSpec(memory_space=vmem),
        scratch_shapes=[vmem(shape, part.dtype) for shape, part in zip(shapes, held)] + [
            vmem((first, parts * 2 * cols), bf16),
            vmem((devs, parts * rows, 2 * cols), bf16),
            vmem((parts * rows, 2 * second), bf16),
            vmem((parts * rows, 2 * second), f32),
            vmem((rows, half), f32), vmem((rows, half), f32),
            vmem((8, half), f32), vmem((8, half), f32),
            vmem((devs, rows, 2 * half), bf16), vmem((first, 2 * half), bf16),
            vmem((devs, 8, 128), f32), vmem((devs, 8, 128), f32),
            vmem((2 * first, second), bf16),
            dma((len(held),)), dma((devs,)), dma((devs,)), dma((2,)), dma((2,)),
            dma((devs,)), dma((devs,)), dma((devs,)), dma((devs,)),
        ],
        compiler_params=pltpu.CompilerParams(
            collective_id=0, has_side_effects=True, vmem_limit_bytes=56 * 1024 * 1024),
    )(cutoff, order, *held)


def fits(strain, bank, devs):
    segs, first, cols = strain.shape
    rows = first // devs
    return (2 * cols == 128 and rows % 16 == 0 and segs % 2 == 0 and devs % 4 == 0
            and bank.shape[1] == devs)


def program(strain, analysis, bank, cutoff, order):
    if fits(strain, bank, lax.axis_size("tmpl")):
        return fused(strain, analysis, bank, cutoff, order)
    return local(strain, analysis, bank, cutoff, order)


def solution(mesh):
    return jax.shard_map(
        program,
        mesh=mesh,
        in_specs=(P("grp", None, "tmpl"), P("grp", "tmpl"), P(None, None, "tmpl", None), P(), P()),
        out_specs=P(("grp", "tmpl"), None, None),
        check_vma=False,
    )
```

```python
import functools
import math

import jax
import jax.numpy as jnp
import numpy as np
from jax import lax
from jax.experimental import pallas as pl
from jax.experimental.pallas import tpu as pltpu
from jax.sharding import PartitionSpec as P


def angles(left_idx, right_idx, period):
    product = left_idx[:, None] * right_idx[None, :] % period
    phase_angle = product.astype(jnp.float32) * (2.0 * math.pi / period)
    return (jnp.cos(phase_angle), jnp.sin(phase_angle))


def filtered(white_pair, tmpl_pair, cut_bins, freq_bin):
    white_real = white_pair[0].astype(jnp.float32)
    white_imag = white_pair[1].astype(jnp.float32)
    tmpl_real = tmpl_pair[0].astype(jnp.float32)
    tmpl_imag = tmpl_pair[1].astype(jnp.float32)
    in_band = freq_bin[None] < cut_bins[:, None, None]
    filt_real = jnp.where(in_band, white_real * tmpl_real + white_imag * tmpl_imag, 0.0)
    filt_imag = jnp.where(in_band, white_imag * tmpl_real - white_real * tmpl_imag, 0.0)
    return jnp.concatenate([filt_real, filt_imag], -1).astype(jnp.bfloat16)


def inverse_rows(stacked, row_bins, second_len, length):
    half_len = second_len // 2
    cosine, sine = angles(
        jnp.arange(half_len, dtype=jnp.int32), jnp.arange(second_len, dtype=jnp.int32), second_len
    )
    dft_table = jnp.concatenate(
        [jnp.concatenate([cosine, sine], 1), jnp.concatenate([-sine, cosine], 1)], 0
    ).astype(jnp.bfloat16)
    spread = jnp.einsum("tkf,fg->tkg", stacked, dft_table, preferred_element_type=jnp.float32)
    spread_real = spread[..., :second_len]
    spread_imag = spread[..., second_len:]
    cos_twist, sin_twist = angles(row_bins, jnp.arange(second_len, dtype=jnp.int32), length)
    lift_real = spread_real * cos_twist - spread_imag * sin_twist
    lift_imag = spread_real * sin_twist + spread_imag * cos_twist
    return jnp.concatenate([lift_real, lift_imag], -1).astype(jnp.bfloat16)


def inverse_cols(lifted, first_len, second_len):
    row_idx = jnp.arange(first_len, dtype=jnp.int32)
    cosine, sine = angles(row_idx, row_idx, first_len)
    cosine = cosine.astype(jnp.bfloat16)
    sine = sine.astype(jnp.bfloat16)
    lift_real = lifted[..., :second_len]
    lift_imag = lifted[..., second_len:]
    field_real = jnp.einsum(
        "ak,tkb->tab", cosine, lift_real, preferred_element_type=jnp.float32
    ) - jnp.einsum("ak,tkb->tab", sine, lift_imag, preferred_element_type=jnp.float32)
    field_imag = jnp.einsum(
        "ak,tkb->tab", sine, lift_real, preferred_element_type=jnp.float32
    ) + jnp.einsum("ak,tkb->tab", cosine, lift_imag, preferred_element_type=jnp.float32)
    return (field_real, field_imag)


def local(strain, analysis, bank, cutoff, order):
    highest = lax.Precision.HIGHEST
    dev_count = lax.axis_size("tmpl")
    my_index = lax.axis_index("tmpl")
    seg_count = strain.shape[0]
    first_len = strain.shape[1]
    col_count = strain.shape[2]
    second_len = col_count * dev_count
    length = first_len * second_len
    half_len = second_len // 2
    row_count = first_len // dev_count
    row_idx = jnp.arange(first_len, dtype=jnp.int32)
    col_index = my_index * col_count + jnp.arange(col_count, dtype=jnp.int32)
    sample_idx = row_idx[:, None] * second_len + col_index[None, :]
    window = (
        math.sqrt(8.0 / 3.0) * jnp.sin(sample_idx.astype(jnp.float32) * (math.pi / length)) ** 2
    )
    series = jnp.concatenate([strain * window, analysis[None]], 0)
    cos_one, sin_one = angles(row_idx, row_idx, first_len)
    part_real = jnp.einsum("ka,sab->skb", cos_one, series, precision=highest)
    part_imag = -jnp.einsum("ka,sab->skb", sin_one, series, precision=highest)
    cos_twist, sin_twist = angles(row_idx, col_index, length)
    twist_real = part_real * cos_twist + part_imag * sin_twist
    twist_imag = part_imag * cos_twist - part_real * sin_twist
    moved = lax.all_to_all(
        jnp.stack([twist_real, twist_imag]).astype(jnp.bfloat16),
        "tmpl",
        split_axis=2,
        concat_axis=3,
        tiled=True,
    ).astype(jnp.float32)
    cos_two, sin_two = angles(
        jnp.arange(second_len, dtype=jnp.int32), jnp.arange(half_len, dtype=jnp.int32), second_len
    )
    spec_real = jnp.einsum("skb,bf->skf", moved[0], cos_two, precision=highest) + jnp.einsum(
        "skb,bf->skf", moved[1], sin_two, precision=highest
    )
    spec_imag = jnp.einsum("skb,bf->skf", moved[1], cos_two, precision=highest) - jnp.einsum(
        "skb,bf->skf", moved[0], sin_two, precision=highest
    )
    power_spec = jnp.maximum(
        jnp.mean(spec_real[:seg_count] ** 2 + spec_imag[:seg_count] ** 2, axis=0), 0.2 * length
    )
    whitened = jnp.stack(
        [spec_real[seg_count] / power_spec, spec_imag[seg_count] / power_spec]
    ).astype(jnp.bfloat16)
    own_rows = my_index * row_count + jnp.arange(row_count, dtype=jnp.int32)
    half_idx = jnp.arange(half_len, dtype=jnp.int32)
    freq_local = own_rows[:, None] + first_len * half_idx[None, :]
    pick = (order[:, None] == jnp.arange(order.shape[0], dtype=jnp.int32)[None, :]).astype(bank.dtype)
    chosen = jnp.einsum("jt,ctkf->cjkf", pick, bank)
    cuts = jnp.take(cutoff, order)
    bank_real = chosen[0].astype(jnp.float32)
    bank_imag = chosen[1].astype(jnp.float32)
    in_band = freq_local[None] < cuts[:, None, None]
    local_norm = jnp.sum(
        jnp.where(in_band, (bank_real**2 + bank_imag**2) / power_spec, 0.0), axis=(1, 2)
    )
    norm_sq = lax.psum(local_norm, "tmpl")
    per_device = cuts.shape[0] // dev_count
    own_norm = lax.dynamic_slice_in_dim(norm_sq, my_index * per_device, per_device)
    stacked = filtered(whitened, chosen, cuts, freq_local)
    lifted = lax.all_to_all(
        inverse_rows(stacked, own_rows, second_len, length),
        "tmpl",
        split_axis=0,
        concat_axis=1,
        tiled=True,
    )
    field_real, field_imag = inverse_cols(lifted, first_len, second_len)
    magnitude = jnp.sqrt(field_real**2 + field_imag**2)
    return (magnitude / jnp.sqrt(own_norm)[:, None, None]).astype(jnp.bfloat16)


GROUP = 4


def unit(left, right, period):
    phase = (left[:, None] * right[None, :] % period) * (2.0 * np.pi / period)
    return np.cos(phase), np.sin(phase)


def tables(devs, first, cols):
    second = cols * devs
    half = second // 2
    length = first * second
    rows = first // devs
    k1 = np.arange(first, dtype=np.int64)
    b = np.arange(second, dtype=np.int64)
    cos, sin = unit(k1, k1, first)
    fwd_one = np.stack([cos.reshape(devs, rows, first), sin.reshape(devs, rows, first)], 1)
    fwd_one = fwd_one.reshape(devs, 2 * rows, first)
    samples = k1[:, None] * second + b[None, :]
    window = np.sqrt(8.0 / 3.0) * np.sin(samples * (np.pi / length)) ** 2
    tcos, tsin = unit(k1, b, length)

    def paired(left, right):
        split = [part.reshape(first, devs, cols).transpose(1, 0, 2) for part in (left, right)]
        return np.concatenate(split, 2)

    window = window.reshape(first, devs, cols).transpose(1, 2, 0)
    twist_cos = paired(tcos, tcos)
    twist_sin = paired(tsin, -tsin)
    low = np.arange(half, dtype=np.int64)
    blocks = []
    for bins in (low, second - 1 - low):
        cos, sin = unit(b, bins, second)
        real = np.concatenate([cos.reshape(devs, cols, half), sin.reshape(devs, cols, half)], 1)
        imag = np.concatenate([-sin.reshape(devs, cols, half), cos.reshape(devs, cols, half)], 1)
        blocks += [real.reshape(2 * second, half), imag.reshape(2 * second, half)]
    fwd_two = np.concatenate(blocks, 1)
    cos, sin = unit(low, b, second)
    inv_one = np.block([[cos, sin], [-sin, cos]])
    cos, sin = unit(k1, k1, first)
    inv_two = np.block([[cos, -sin], [sin, cos]]).reshape(2 * first, 2, devs // GROUP, GROUP * rows)
    inv_two = inv_two.transpose(2, 0, 1, 3).reshape(devs // GROUP, 2 * first, 2 * GROUP * rows)
    found = (fwd_one, window, twist_cos, twist_sin, fwd_two, inv_one, tcos, tsin, inv_two)
    return [part.astype(np.float32).astype(jnp.bfloat16) for part in found]


def kernel(
    devs, group,
    cutoff, order, strain_h, analysis_h, bank_h, one_h, window_h, tcos_h, tsin_h, two_h, inv_h, ucos_h, usin_h, last_h,
    out,
    strain, analysis, bank, one, window, tcos, tsin, two, inv, ucos, usin, last,
    series, send_a, recv_a, spec, mirror_out, mirror_in, edge_out, edge_in, send_q, recv_q, norm_out, norm_in, lifted, total,
    load_sem, a_send, a_recv, m_send, m_recv, q_send, q_recv, n_send, n_recv,
):
    f32, bf16 = jnp.float32, jnp.bfloat16
    me = lax.axis_index("tmpl")
    segs, cols, first = strain.shape
    pairs = segs // 2
    width = 2 * cols
    rows = first // devs
    second = cols * devs
    half = second // 2
    length = first * second
    packed = pairs * rows

    loads = []
    for at, (src, dst) in enumerate([
        (strain_h, strain), (analysis_h, analysis), (window_h.at[me], window), (one_h, one),
        (tcos_h.at[me], tcos), (tsin_h.at[me], tsin), (two_h, two), (bank_h, bank),
        (inv_h, inv), (ucos_h, ucos), (usin_h, usin), (last_h, last),
    ]):
        loads.append(pltpu.make_async_copy(src, dst, load_sem.at[at]))
    for copy in loads[:6]:
        copy.start()

    barrier = pltpu.get_barrier_semaphore()

    def greet(step, carry):
        pl.semaphore_signal(barrier, inc=1, device_id={"tmpl": lax.rem(me + step, devs)},
                            device_id_type=pl.DeviceIdType.MESH)
        return carry

    lax.fori_loop(1, devs, greet, 0)

    for copy in loads[:3]:
        copy.wait()
    for seg in range(segs):
        series[seg * cols:(seg + 1) * cols, :] = (strain[seg] * window[...].astype(f32)).astype(bf16)
    series[segs * cols:(segs + 1) * cols, :] = analysis[...].astype(bf16)
    series[(segs + 1) * cols:, :] = jnp.zeros((cols, first), bf16)
    for copy in loads[3:6]:
        copy.wait()
    for copy in loads[6:]:
        copy.start()
    lane = lax.broadcasted_iota(jnp.int32, (rows, width), 1)
    sign = jnp.where(lane < cols, -1.0, 1.0)

    pl.semaphore_wait(barrier, devs - 1)

    def a_copy(peer, source):
        return pltpu.make_async_remote_copy(
            src_ref=send_a.at[peer],
            dst_ref=recv_a.at[:, pl.ds(pl.multiple_of(source * width, width), width)],
            send_sem=a_send.at[peer], recv_sem=a_recv.at[source],
            device_id={"tmpl": peer}, device_id_type=pl.DeviceIdType.MESH)

    own_set = me // group
    sets = devs // group

    def spread(step, carry):
        chunk = lax.rem(own_set + 1 + step, sets)
        part = lax.dot_general(one[pl.ds(chunk * group, group)].reshape(group * 2 * rows, first), series[...],
                               (((1,), (1,)), ((), ())), preferred_element_type=f32)
        for member in range(group):
            peer = chunk * group + member
            at = pl.ds(pl.multiple_of(peer * rows, rows), rows)
            cos, sin = tcos[at, :].astype(f32), tsin[at, :].astype(f32)
            base = member * 2 * rows
            for seg in range(pairs + 1):
                upper = part[base:base + rows, seg * width:(seg + 1) * width]
                lower = part[base + rows:base + 2 * rows, seg * width:(seg + 1) * width]
                field = upper + pltpu.roll(lower * sign, cols, 1)
                field = field * cos + pltpu.roll(field, cols, 1) * sin
                send_a[peer, seg * rows:(seg + 1) * rows, :] = field.astype(bf16)

            @pl.when(peer != me)
            def _():
                a_copy(peer, me).start()
        return carry

    lax.fori_loop(0, sets, spread, 0)
    recv_a[:, pl.ds(pl.multiple_of(me * width, width), width)] = send_a[me]
    loads[6].wait()
    spec[...] = jnp.zeros(spec.shape, f32)
    total[...] = jnp.zeros(total.shape, f32)

    def others(body):
        def step(at, carry):
            body(lax.rem(me + at, devs))
            return carry
        lax.fori_loop(1, devs, step, 0)

    chunk_cols = min(half, 512)
    deep = group * width

    def gather(step, carry):
        chunk = lax.rem(own_set + sets - 1 - step, sets)
        for member in range(group):
            peer = chunk * group + member

            @pl.when(peer != me)
            def _():
                a_copy(peer, peer).wait_recv()
        block = pl.ds(pl.multiple_of(chunk * deep, deep), deep)

        def columns(tile, inner):
            at = pl.ds(pl.multiple_of(tile * chunk_cols, chunk_cols), chunk_cols)
            spec[:, at] += jnp.dot(recv_a[:, block], two[block, at], preferred_element_type=f32)
            return inner

        return lax.fori_loop(0, 2 * second // chunk_cols, columns, carry)

    lax.fori_loop(0, sets, gather, 0)

    def power(start):
        found = jnp.zeros((rows, half), f32)
        for pair in range(pairs):
            for part in (start, start + half):
                value = spec[pair * rows:(pair + 1) * rows, part:part + half]
                found = found + value * value
        return found

    far = power(second)
    near_row = lax.broadcasted_iota(jnp.int32, (rows, rows), 0)
    near_col = lax.broadcasted_iota(jnp.int32, (rows, rows), 1)
    flip = jnp.where(near_row + near_col == rows, 1.0, 0.0)
    mirror_out[...] = jnp.dot(flip, far, preferred_element_type=f32, precision=lax.Precision.HIGHEST)
    edge_out[...] = far[:8]
    partner = devs - 1 - me
    edge_partner = lax.rem(devs - me, devs)
    mirror_copy = pltpu.make_async_remote_copy(
        src_ref=mirror_out, dst_ref=mirror_in, send_sem=m_send.at[0], recv_sem=m_recv.at[0],
        device_id={"tmpl": partner}, device_id_type=pl.DeviceIdType.MESH)
    edge_copy = pltpu.make_async_remote_copy(
        src_ref=edge_out, dst_ref=edge_in, send_sem=m_send.at[1], recv_sem=m_recv.at[1],
        device_id={"tmpl": edge_partner}, device_id_type=pl.DeviceIdType.MESH)
    mirror_copy.start()

    @pl.when(edge_partner != me)
    def _():
        edge_copy.start()
    close = power(0)

    @pl.when(edge_partner == me)
    def _():
        edge_lane = lax.broadcasted_iota(jnp.int32, (8, half), 1)
        shifted = jnp.where(edge_lane == 0, close[:8], pltpu.roll(far[:8], 1, 1))
        edge_in[...] = jnp.where(me == 0, shifted, far[:8])

    @pl.when(edge_partner != me)
    def _():
        edge_copy.wait_recv()
    mirror_copy.wait_recv()
    row = lax.broadcasted_iota(jnp.int32, (rows, half), 0)
    opposite = jnp.where(row == 0, edge_in[0:1, :], mirror_in[...])
    inverse = 1.0 / jnp.maximum((close + opposite) * (0.5 / segs), 0.2 * length)
    white_real = (spec[packed:, :half] * inverse).astype(bf16).astype(f32)
    white_imag = (spec[packed:, half:second] * inverse).astype(bf16).astype(f32)
    freq = me * rows + row + first * lax.broadcasted_iota(jnp.int32, (rows, half), 1)
    loads[7].wait()

    def q_copy(peer, source):
        return pltpu.make_async_remote_copy(
            src_ref=send_q.at[peer],
            dst_ref=recv_q.at[pl.ds(pl.multiple_of(source * rows, rows), rows), :],
            send_sem=q_send.at[peer], recv_sem=q_recv.at[source],
            device_id={"tmpl": peer}, device_id_type=pl.DeviceIdType.MESH)

    def n_copy(peer, source):
        return pltpu.make_async_remote_copy(
            src_ref=norm_out.at[peer], dst_ref=norm_in.at[source],
            send_sem=n_send.at[peer], recv_sem=n_recv.at[source],
            device_id={"tmpl": peer}, device_id_type=pl.DeviceIdType.MESH)

    def filters(step, carry):
        peer = lax.rem(own_set + 1 + step // group, sets) * group + lax.rem(step + me, group)
        which = order[peer]
        inside = freq < cutoff[which]
        real, imag = bank[0, which].astype(f32), bank[1, which].astype(f32)
        send_q[peer, :, :half] = jnp.where(inside, white_real * real + white_imag * imag, 0.0).astype(bf16)
        send_q[peer, :, half:] = jnp.where(inside, white_imag * real - white_real * imag, 0.0).astype(bf16)
        weight = jnp.where(inside, (real * real + imag * imag) * inverse, 0.0)
        folded = sum(weight[at:at + 8] for at in range(0, rows, 8))
        norm_out[peer] = sum(folded[:, at:at + 128] for at in range(0, half, 128))

        @pl.when(peer != me)
        def _():
            q_copy(peer, me).start()
            n_copy(peer, me).start()
        return carry

    lax.fori_loop(0, devs, filters, 0)
    recv_q[pl.ds(pl.multiple_of(me * rows, rows), rows), :] = send_q[me]
    norm_in[me] = norm_out[me]
    for copy in loads[8:]:
        copy.wait()

    tail = 256
    tall = group * rows

    def rows_back(step):
        chunk = lax.rem(own_set + sets - 1 - step, sets)
        for member in range(group):
            peer = chunk * group + member

            @pl.when(peer != me)
            def _():
                q_copy(peer, peer).wait_recv()
        at = pl.ds(pl.multiple_of(chunk * tall, tall), tall)
        wide = jnp.dot(recv_q[at, :], inv[...], preferred_element_type=f32)
        real, imag = wide[:, :second], wide[:, second:]
        cos, sin = ucos[at, :].astype(f32), usin[at, :].astype(f32)
        lifted[:tall, :] = (real * cos - imag * sin).astype(bf16)
        lifted[tall:, :] = (real * sin + imag * cos).astype(bf16)
        return chunk

    def back(step, carry):
        chunk = rows_back(step)

        def cols_back(tile, inner):
            at = pl.ds(pl.multiple_of(tile * tail, tail), tail)
            total[:, at] += jnp.dot(last[chunk], lifted[:, at], preferred_element_type=f32)
            return inner

        return lax.fori_loop(0, second // tail, cols_back, carry)

    lax.fori_loop(0, sets - 1, back, 0)
    others(lambda peer: n_copy(peer, peer).wait_recv())
    norm = jnp.sum(jnp.sum(jnp.sum(norm_in[...], 0), 0, keepdims=True), 1, keepdims=True)
    gain = 1.0 / jnp.sqrt(norm)
    chunk = rows_back(sets - 1)

    def finish(tile, carry):
        at = pl.ds(pl.multiple_of(tile * tail, tail), tail)
        field = total[:, at] + jnp.dot(last[chunk], lifted[:, at], preferred_element_type=f32)
        real, imag = field[:first], field[first:]
        out[0, :, at] = (jnp.sqrt(real * real + imag * imag) * gain).astype(bf16)
        return carry

    lax.fori_loop(0, second // tail, finish, 0)

    def drain(peer):
        a_copy(peer, me).wait_send()
        q_copy(peer, me).wait_send()
        n_copy(peer, me).wait_send()

    others(drain)
    mirror_copy.wait_send()

    @pl.when(edge_partner != me)
    def _():
        edge_copy.wait_send()


def fused(strain, analysis, bank, cutoff, order):
    devs = lax.axis_size("tmpl")
    segs, first, cols = strain.shape
    second = cols * devs
    half = second // 2
    rows = first // devs
    group = GROUP
    parts = segs // 2 + 1
    f32, bf16 = jnp.float32, jnp.bfloat16
    consts = [jnp.asarray(part) for part in tables(devs, first, cols)]
    smem = pl.BlockSpec(memory_space=pltpu.SMEM)
    held = [strain.transpose(0, 2, 1), analysis.T, bank] + consts
    shapes = [part.shape for part in held]
    for at in (4, 5, 6):
        shapes[at] = shapes[at][1:]
    vmem = pltpu.VMEM
    dma = pltpu.SemaphoreType.DMA
    return pl.pallas_call(
        functools.partial(kernel, devs, group),
        out_shape=jax.ShapeDtypeStruct((1, first, second), bf16),
        in_specs=[smem, smem] + [pl.BlockSpec(memory_space=pl.ANY)] * len(held),
        out_specs=pl.BlockSpec(memory_space=vmem),
        scratch_shapes=[vmem(shape, part.dtype) for shape, part in zip(shapes, held)] + [
            vmem((parts * 2 * cols, first), bf16),
            vmem((devs, parts * rows, 2 * cols), bf16),
            vmem((parts * rows, 2 * second), bf16),
            vmem((parts * rows, 2 * second), f32),
            vmem((rows, half), f32), vmem((rows, half), f32),
            vmem((8, half), f32), vmem((8, half), f32),
            vmem((devs, rows, 2 * half), bf16), vmem((first, 2 * half), bf16),
            vmem((devs, 8, 128), f32), vmem((devs, 8, 128), f32),
            vmem((2 * group * rows, second), bf16), vmem((2 * first, second), f32),
            dma((len(held),)), dma((devs,)), dma((devs,)), dma((2,)), dma((2,)),
            dma((devs,)), dma((devs,)), dma((devs,)), dma((devs,)),
        ],
        compiler_params=pltpu.CompilerParams(
            collective_id=0, has_side_effects=True, vmem_limit_bytes=56 * 1024 * 1024),
    )(cutoff, order, *held)


def fits(strain, bank, devs):
    segs, first, cols = strain.shape
    rows = first // devs
    return (2 * cols == 128 and rows % 16 == 0 and segs % 2 == 0 and devs % GROUP == 0
            and bank.shape[1] == devs)


def program(strain, analysis, bank, cutoff, order):
    if fits(strain, bank, lax.axis_size("tmpl")):
        return fused(strain, analysis, bank, cutoff, order)
    return local(strain, analysis, bank, cutoff, order)


def solution(mesh):
    return jax.shard_map(
        program,
        mesh=mesh,
        in_specs=(P("grp", None, "tmpl"), P("grp", "tmpl"), P(None, None, "tmpl", None), P(), P()),
        out_specs=P(("grp", "tmpl"), None, None),
        check_vma=False,
    )
```
